32 devices in a mesh: row: 8 (over y, x, core), col: 4 (over z).
Axes of the slice: x: 2, y: 2, z: 4, core: 2. Of those that a mesh axis runs over, the one named last changes fastest.
Arguments:
- draws: bfloat16 [128, 16384], P('row', 'col'), may hold values from -6 to 6
- u_factors: bfloat16 [16, 16, 1024, 64], P('row', 'col'), may hold values from -0.1875 to 0.1875
- v_factors: bfloat16 [16, 16, 1024, 64], P('row', 'col'), may hold values from -0.1875 to 0.1875
- ranks: int32 [16, 16], P('row', 'col'), may hold values from 16 to 64
- near: int32 [16, 16], P('row'), may hold values from 0 to 15, as said below
- row_coords: float32 [2, 16384], P(None, 'row'), may hold values from 0 to 4
- col_coords: float32 [2, 16384], replicated, may hold values from 0 to 4
Outputs:
- applied: float32 [128, 16384], P('col', 'row')
The draws below stay inside these ranges and needn't reach their ends.
Inputs may be any that keep to these rules, and one draw needn't show every extreme that they name: `ranks`: the rank of a tile; factor columns from its rank on are padding. `near`: each block row lists 16 different block columns.
All inputs are finite; a program needn't handle non-finite values.
Results may differ from the reference program's by a relative error of at most 0.0029.
Values may be sent and summed in bfloat16 or wider, within the bound.
A program may use at most 64 MiB of HBM per device.

```python
import jax
import jax.numpy as jnp
from jax import lax

TILE = 1024
RANK = 64
NRHS = 128
NEAR = 16
BR = 16
BC = 16


def cell_place(index):
    column = index // 4
    within = index % 4
    upward = jnp.where(column % 2 == 0, within, 3 - within)
    return (column, upward)


def row_cells(key):
    first, second, third, fourth = jax.random.split(key, 4)
    spot = jax.random.randint(first, (), 0, BC)
    beside_all = jax.random.randint(second, (BR,), 0, min(12, BC))
    spread = jax.random.randint(third, (BR,), 0, BC)
    pick = jax.random.randint(fourth, (BR,), 0, 2)
    return jnp.where(pick == 1, (spot + beside_all) % BC, spread).astype(jnp.int32)


def draw_near(key, part):
    cells = row_cells(jax.random.fold_in(key, 7))
    row_x, row_y = cell_place(cells)
    column_ids = jnp.arange(BC, dtype=jnp.int32)
    col_x, col_y = cell_place(column_ids)
    delta_x = row_x[:, None] - col_x[None, :]
    delta_y = row_y[:, None] - col_y[None, :]
    squared = delta_x * delta_x + delta_y * delta_y
    offset = jax.random.randint(jax.random.fold_in(key, 9), (BR, 1), 0, BC)
    score = squared * BC + (column_ids[None, :] + offset) % BC
    values, picked = lax.top_k(-score, NEAR)
    return picked.astype(jnp.int32)


def draw_row_coords(key, part):
    cells = row_cells(jax.random.fold_in(key, 7))
    site_cells = jnp.repeat(cells, TILE)
    cell_x, cell_y = cell_place(site_cells)
    jitter = jax.random.uniform(jax.random.fold_in(key, 13), (2, BR * TILE), jnp.float32)
    return jnp.stack([cell_x, cell_y]).astype(jnp.float32) + jitter


def draw_col_coords(key, part):
    site_cells = jnp.arange(BC * TILE, dtype=jnp.int32) // TILE
    cell_x, cell_y = cell_place(site_cells)
    jitter = jax.random.uniform(jax.random.fold_in(key, 11), (2, BC * TILE), jnp.float32)
    return jnp.stack([cell_x, cell_y]).astype(jnp.float32) + jitter


def plant(array, stream_key, low, top_value):
    longest = array.shape.index(max(array.shape))
    spots = []
    for shift in (0, 1):
        where = [jax.random.randint(jax.random.fold_in(stream_key, axis), (), 0, length) for axis, length in enumerate(array.shape)]
        where[longest] = (where[longest] + shift) % array.shape[longest]
        spots.append(tuple(where))
    return array.at[spots[0]].set(low).at[spots[1]].set(top_value)


def level_of(own_key, extent, pieces, low, largest):
    def one(axis_at, shards_of):
        steps = jax.random.uniform(jax.random.fold_in(jax.random.fold_in(own_key, 6), axis_at), (shards_of,), jnp.float32, low / len(pieces), largest / len(pieces))
        return jnp.repeat(jnp.exp(steps), extent[axis_at] // shards_of).reshape((-1,) + (1,) * (len(extent) - axis_at - 1))

    factor_of = one(*pieces[0])
    for cut in pieces[1:]:
        factor_of = factor_of * one(*cut)
    return factor_of


def normal_values(own_key, shape, deviation, most, cuts=(), kind=jnp.bfloat16):
    loudness = level_of(own_key, shape, cuts, -0.22, 0.18) if cuts else 1.0
    drawn = jax.random.normal(own_key, shape, jnp.float32) * deviation * loudness
    return jnp.minimum(jnp.maximum(drawn, -most), most).astype(kind)


def setup_inputs(seed: int = 0) -> dict:
    keys = jax.random.split(jax.random.key(seed), 8)
    draws = normal_values(keys[0], (NRHS, BC * TILE), 1.0, 6.0, ((0, 8), (1, 4)))
    u_factors = normal_values(keys[1], (BR, BC, TILE, RANK), (RANK * BC) ** -0.5, 0.1875, ((0, 8), (1, 4)))
    v_factors = normal_values(keys[2], (BR, BC, TILE, RANK), TILE ** -0.5, 0.1875, ((0, 8), (1, 4)))
    ranks = plant(jax.random.randint(keys[3], (BR, BC), RANK // 4, RANK + 1), jax.random.fold_in(keys[3], 1), RANK // 4, RANK).astype(jnp.int32)
    near = draw_near(jax.random.fold_in(keys[7], 71), 0)
    row_coords = draw_row_coords(jax.random.fold_in(keys[7], 71), 0)
    col_coords = draw_col_coords(jax.random.fold_in(keys[7], 71), 0)
    return {"draws": draws, "u_factors": u_factors, "v_factors": v_factors, "ranks": ranks, "near": near, "row_coords": row_coords, "col_coords": col_coords}


def matern_tile(col_part, row_part):
    delta_x = col_part[0][:, None] - row_part[0][None, :]
    delta_y = col_part[1][:, None] - row_part[1][None, :]
    kernel = jnp.exp(-jnp.sqrt(delta_x * delta_x + delta_y * delta_y)) * 0.03125
    return kernel.astype(jnp.bfloat16)

def reference(draws, u_factors, v_factors, ranks, near, row_coords, col_coords):
    blocks = draws.reshape(NRHS, BC, TILE).astype(jnp.float32)
    column_ids = jnp.arange(BC, dtype=jnp.int32)
    flagged = jnp.any(near[:, :, None] == column_ids[None, None, :], axis=1)
    rank_ids = jnp.arange(RANK, dtype=jnp.int32)

    def one_row(index):
        v_row = v_factors[index].astype(jnp.float32)
        u_row = u_factors[index].astype(jnp.float32)
        reduced = jnp.einsum('nbt,btk->nbk', blocks, v_row)
        keep = (rank_ids[None, :] < ranks[index][:, None]) & jnp.logical_not(flagged[index])[:, None]
        reduced = jnp.where(keep[None], reduced, 0.0).astype(jnp.bfloat16).astype(jnp.float32)
        total = jnp.einsum('nbk,btk->nt', reduced, u_row)
        row_part = lax.dynamic_slice_in_dim(row_coords, (index * TILE).astype(jnp.int32), TILE, 1)

        def add_slot(slot, acc):
            column = near[index, slot].astype(jnp.int32)
            tile_matrix = matern_tile(lax.dynamic_slice_in_dim(col_coords, column * TILE, TILE, 1), row_part)
            piece = lax.dynamic_slice_in_dim(draws, column * TILE, TILE, 1)
            return acc + jnp.dot(piece, tile_matrix, preferred_element_type=jnp.float32)
        return lax.fori_loop(0, NEAR, add_slot, total)
    rows_out = lax.map(one_row, jnp.arange(BR, dtype=jnp.int32))
    return jnp.transpose(rows_out, (1, 0, 2)).reshape(NRHS, BR * TILE)
```

```python
import functools

import jax
import jax.numpy as jnp
from jax import lax
from jax.experimental import pallas as pl
from jax.experimental.pallas import tpu as pltpu
from jax.sharding import PartitionSpec as P

MESH = pl.DeviceIdType.MESH
LOG2E = 1.4426950408889634
TINY = 1e-12
WIDE = 256
TERMS = 32


def matern_tile(col_part, row_part):
    delta_x = col_part[0][:, None] - row_part[0][None, :]
    delta_y = col_part[1][:, None] - row_part[1][None, :]
    kernel = jnp.exp(-jnp.sqrt(delta_x * delta_x + delta_y * delta_y)) * 0.03125
    return kernel.astype(jnp.bfloat16)


def per_device(draws, u_factors, v_factors, ranks, near, row_coords, col_coords):
    rows_local, cols_local, tile, rank = u_factors.shape
    first_col = lax.axis_index("col") * cols_local
    whole = lax.all_gather(draws, "row", axis=0, tiled=True)
    width = whole.shape[0]
    column_ids = first_col + jnp.arange(cols_local, dtype=jnp.int32)
    flagged = jnp.any(near[:, :, None] == column_ids[None, None, :], axis=1)
    keep = (jnp.arange(rank, dtype=jnp.int32)[None, None, :] < ranks[:, :, None]) & jnp.logical_not(
        flagged
    )[:, :, None]
    blocks = whole.reshape(width, cols_local, tile)
    reduced = jnp.einsum("nbt,abtk->nabk", blocks, v_factors, preferred_element_type=jnp.float32)
    reduced = jnp.where(keep[None], reduced, 0.0).astype(jnp.bfloat16)
    partial_value = jnp.einsum(
        "nabk,abtk->nat", reduced, u_factors, preferred_element_type=jnp.float32
    )
    partial_value = partial_value.reshape(width, rows_local * tile)
    local_cols = lax.dynamic_slice_in_dim(col_coords, first_col * tile, cols_local * tile, 1)

    def add_tile(step, total):
        row_pos = step // cols_local
        col_pos = step % cols_local

        def dense(acc):
            tile_matrix = matern_tile(
                lax.dynamic_slice_in_dim(local_cols, col_pos * tile, tile, 1),
                lax.dynamic_slice_in_dim(row_coords, row_pos * tile, tile, 1),
            )
            piece = lax.dynamic_slice_in_dim(whole, col_pos * tile, tile, 1)
            product = jnp.dot(piece, tile_matrix, preferred_element_type=jnp.float32)
            current = lax.dynamic_slice_in_dim(acc, row_pos * tile, tile, 1)
            return lax.dynamic_update_slice_in_dim(acc, current + product, row_pos * tile, 1)

        return lax.cond(flagged[row_pos, col_pos], dense, lambda acc: acc, total)

    partial_value = lax.fori_loop(0, rows_local * cols_local, add_tile, partial_value)
    result = lax.psum_scatter(partial_value, "col", scatter_dimension=0, tiled=True)
    return result


def split3(value):
    high = value.astype(jnp.bfloat16).astype(jnp.float32)
    rest = value - high
    middle = rest.astype(jnp.bfloat16).astype(jnp.float32)
    return high, middle, rest - middle


def write_terms(target, coords, is_row):
    target[...] = jnp.zeros_like(target)
    x = (coords[0:1, :] - 2.0) * LOG2E
    y = (coords[1:2, :] - 2.0) * LOG2E
    norm = split3(x * x + y * y)
    at = 0
    order = (0, 1, 0, 2, 0, 1) if is_row else (0, 0, 1, 0, 2, 1)
    for value in (x, y):
        parts = split3(value)
        for piece in order:
            target[at : at + 1, :] = parts[piece] * -2.0 if is_row else parts[piece]
            at += 1
    ones = jnp.ones_like(x)
    for piece in range(3):
        target[at : at + 1, :] = ones if is_row else norm[piece]
        target[at + 3 : at + 4, :] = norm[piece] if is_row else ones
        at += 1


def kernel(
    cols, draws, u_hbm, v_hbm, ranks, near, row_coords, col_coords, out,
    u, v, whole, dense, col_terms, col_left, row_terms, red, total, mail, inbox, own,
    factor_sem, gs_sem, gr_sem, ss_sem, sr_sem,
):
    groups, part_rows, width = whole.shape[0], whole.shape[1], whole.shape[2]
    rows_local, cols_local, tile, rank = u.shape
    nrhs = groups * part_rows
    share = nrhs // cols
    chunks = rows_local * tile // WIDE
    per_row = tile // WIDE
    row = lax.axis_index("row")
    col = lax.axis_index("col")
    first = col * cols_local

    sibling = row + 1 - 2 * (row % 2)
    beside = row + 2 - 4 * ((row // 2) % 2)
    above = row + 4 - 8 * ((row // 4) % 2)
    across = beside + 4 - 8 * ((row // 4) % 2)

    def other(index):
        return index + 1 - 2 * (index % 2)

    barrier = pltpu.get_barrier_semaphore()
    for peer in (sibling, beside, above, across):
        pl.semaphore_signal(barrier, inc=1, device_id=(peer, col), device_id_type=MESH)
    for step in range(1, cols):
        pl.semaphore_signal(barrier, inc=1, device_id=(row, (col + step) % cols), device_id_type=MESH)

    u_copy = pltpu.make_async_copy(u_hbm, u, factor_sem.at[0])
    v_copy = pltpu.make_async_copy(v_hbm, v, factor_sem.at[1])
    u_copy.start()
    v_copy.start()

    write_terms(col_terms, col_coords[:, pl.ds(pl.multiple_of(first * tile, tile), width)], False)
    write_terms(row_terms, row_coords[...], True)
    for block in range(width // WIDE):
        span = slice(block * WIDE, (block + 1) * WIDE)
        col_left[span, :] = jnp.transpose(col_terms[:, span]).astype(jnp.bfloat16)
    whole[row] = draws[...]
    pl.semaphore_wait(barrier, 3 + cols)

    def gather(source, slot, peer, index):
        return pltpu.make_async_remote_copy(
            src_ref=source, dst_ref=whole.at[slot], send_sem=gs_sem.at[index],
            recv_sem=gr_sem.at[index], device_id=(peer, col), device_id_type=MESH,
        )

    firsts = [gather(draws, row, peer, index) for index, peer in enumerate((beside, above, across, sibling))]
    for copy in firsts:
        copy.start()

    def gen(chunk, j, quarter):
        right = row_terms[:, chunk * WIDE : (chunk + 1) * WIDE].astype(jnp.bfloat16)
        for half in range(2):
            at = pl.multiple_of(j * tile + quarter * WIDE + half * 128, 128)
            squared = jnp.dot(col_left[pl.ds(at, 128), :], right, preferred_element_type=jnp.float32)
            squared = jnp.maximum(squared, TINY)
            value = jnp.exp2(-(squared * lax.rsqrt(squared)))
            dense[chunk, pl.ds(at, 128), :] = value.astype(jnp.bfloat16)

    def flag(i, j):
        hit = jnp.where(near[i : i + 1, :] == first + j, 1.0, 0.0)
        return jnp.max(hit, axis=1, keepdims=True)

    def mul(chunk, j, quarter):
        at = pl.multiple_of(j * tile + quarter * WIDE, WIDE)
        left = whole[:, :, pl.ds(at, WIDE)].reshape(nrhs, WIDE)
        return jnp.dot(left, dense[chunk, pl.ds(at, WIDE), :], preferred_element_type=jnp.float32)

    def step(makes, takes):
        for take in takes:
            total[take % 2] = jnp.zeros_like(total[take % 2])

        def body(j, carry):
            sums = [None for _ in takes]
            for quarter in range(tile // WIDE):
                for make in makes:
                    gen(make, j, quarter)
                for n, take in enumerate(takes):
                    product = mul(take, j, quarter)
                    sums[n] = product if sums[n] is None else sums[n] + product
            for n, take in enumerate(takes):
                total[take % 2] += sums[n] * flag(take // per_row, j)
            return carry

        lax.fori_loop(0, cols_local, body, 0)
        for take in takes:
            send(take)

    def delivery(chunk, step):
        peer = (col + step) % cols
        return pltpu.make_async_remote_copy(
            src_ref=mail.at[chunk, peer], dst_ref=inbox.at[chunk, step - 1],
            send_sem=ss_sem.at[chunk, step - 1], recv_sem=sr_sem.at[chunk, step - 1],
            device_id=(row, peer), device_id_type=MESH,
        )

    def send(chunk):
        i = chunk // per_row
        base = (chunk % per_row) * WIDE
        value = total[chunk % 2] * 0.03125
        for j in range(cols_local):
            value = value + lax.dot_general(
                red[i, j], u[i, j, base : base + WIDE, :], (((1,), (1,)), ((), ())),
                preferred_element_type=jnp.float32,
            )
        value = value.reshape(cols, share, WIDE)
        mail[chunk] = value.astype(jnp.bfloat16)
        own[chunk] = value
        for step in range(1, cols):
            delivery(chunk, step).start()

    def receive(chunk):
        value = own[chunk, col]
        for step in range(1, cols):
            delivery(chunk, step).wait_recv()
            value = value + inbox[chunk, step - 1].astype(jnp.float32)
        out[:, chunk * WIDE : (chunk + 1) * WIDE] = value

    for phase in PLAN:
        kind = phase[0]
        if kind == "step":
            step(phase[1], phase[2])
        elif kind == "forward":
            for index in phase[1]:
                firsts[index].wait_recv()
                slot = (beside, above, across)[index]
                gather(whole.at[slot], slot, sibling, 4 + index).start()
        elif kind == "ready":
            for index in range(3):
                slot = other((beside, above, across)[index])
                gather(whole.at[slot], slot, sibling, 4 + index).wait_recv()
            firsts[3].wait_recv()
        elif kind == "reduce":
            u_copy.wait()
            v_copy.wait()
            for j in range(cols_local):
                left = whole[:, :, j * tile : (j + 1) * tile].reshape(nrhs, tile)
                for i in range(rows_local):
                    value = jnp.dot(left, v[i, j], preferred_element_type=jnp.float32)
                    index = lax.broadcasted_iota(jnp.int32, value.shape, 1)
                    keep = jnp.where(index < ranks[i : i + 1, j : j + 1], 1.0, 0.0) * (1.0 - flag(i, j))
                    red[i, j] = jnp.where(keep > 0.5, value, 0.0).astype(jnp.bfloat16)
        elif kind == "receive":
            for chunk in phase[1]:
                receive(chunk)

    for copy in firsts:
        copy.wait_send()
    for index in range(3):
        slot = (beside, above, across)[index]
        gather(whole.at[slot], slot, sibling, 4 + index).wait_send()
    for chunk in range(chunks):
        for step_at in range(1, cols):
            delivery(chunk, step_at).wait_send()


PLAN = (
    ("step", (0,), ()),
    ("step", (1,), ()),
    ("forward", (0, 1)),
    ("step", (2,), ()),
    ("forward", (2,)),
    ("step", (3,), ()),
    ("ready",),
    ("reduce",),
    ("step", (4,), (0, 1)),
    ("step", (5,), (2, 3)),
    ("step", (6,), (4, 5)),
    ("receive", (0, 1)),
    ("step", (7,), (6,)),
    ("receive", (2, 3)),
    ("step", (), (7,)),
    ("receive", (4, 5, 6, 7)),
)


def fused(rows, cols, draws, u_factors, v_factors, ranks, near, row_coords, col_coords):
    part_rows, width = draws.shape
    rows_local, cols_local, tile, rank = u_factors.shape
    nrhs = part_rows * rows
    share = nrhs // cols
    chunks = rows_local * tile // WIDE
    vmem = pl.BlockSpec(memory_space=pltpu.VMEM)
    hbm = pl.BlockSpec(memory_space=pl.ANY)
    return pl.pallas_call(
        functools.partial(kernel, cols),
        out_shape=jax.ShapeDtypeStruct((share, rows_local * tile), jnp.float32),
        in_specs=[vmem, hbm, hbm, vmem, vmem, vmem, vmem],
        out_specs=vmem,
        scratch_shapes=[
            pltpu.VMEM(u_factors.shape, jnp.bfloat16),
            pltpu.VMEM(v_factors.shape, jnp.bfloat16),
            pltpu.VMEM((rows, part_rows, width), jnp.bfloat16),
            pltpu.VMEM((chunks, width, WIDE), jnp.bfloat16),
            pltpu.VMEM((TERMS, width), jnp.float32),
            pltpu.VMEM((width, TERMS), jnp.bfloat16),
            pltpu.VMEM((TERMS, rows_local * tile), jnp.float32),
            pltpu.VMEM((rows_local, cols_local, nrhs, rank), jnp.bfloat16),
            pltpu.VMEM((2, nrhs, WIDE), jnp.float32),
            pltpu.VMEM((chunks, cols, share, WIDE), jnp.bfloat16),
            pltpu.VMEM((chunks, cols - 1, share, WIDE), jnp.bfloat16),
            pltpu.VMEM((chunks, cols, share, WIDE), jnp.float32),
            pltpu.SemaphoreType.DMA((2,)),
            pltpu.SemaphoreType.DMA((7,)),
            pltpu.SemaphoreType.DMA((7,)),
            pltpu.SemaphoreType.DMA((chunks, cols - 1)),
            pltpu.SemaphoreType.DMA((chunks, cols - 1)),
        ],
        compiler_params=pltpu.CompilerParams(
            collective_id=0, has_side_effects=True, vmem_limit_bytes=48 * 1024 * 1024
        ),
        cost_estimate=pl.CostEstimate(flops=10**10, bytes_accessed=10**7, transcendentals=2 * 10**7),
    )(draws, u_factors, v_factors, ranks, near, row_coords, col_coords)


def solution(mesh):
    rows, cols = mesh.shape["row"], mesh.shape["col"]

    def local(*args):
        share = args[0].shape[0] * rows // cols
        if rows == 8 and cols == 4 and args[0].shape[0] % 16 == 0 and share % 16 == 0 and args[1].shape[:3] == (2, 4, 1024):
            return fused(rows, cols, *args)
        return per_device(*args)

    return jax.shard_map(
        local,
        mesh=mesh,
        in_specs=(
            P("row", "col"),
            P("row", "col", None, None),
            P("row", "col", None, None),
            P("row", "col"),
            P("row", None),
            P(None, "row"),
            P(),
        ),
        out_specs=P("col", "row"),
        check_vma=False,
    )
```

```python
import functools

import jax
import jax.numpy as jnp
from jax import lax
from jax.experimental import pallas as pl
from jax.experimental.pallas import tpu as pltpu
from jax.sharding import PartitionSpec as P

MESH = pl.DeviceIdType.MESH
LOG2E = 1.4426950408889634
TINY = 1e-12
WIDE = 256


def matern_tile(col_part, row_part):
    delta_x = col_part[0][:, None] - row_part[0][None, :]
    delta_y = col_part[1][:, None] - row_part[1][None, :]
    kernel = jnp.exp(-jnp.sqrt(delta_x * delta_x + delta_y * delta_y)) * 0.03125
    return kernel.astype(jnp.bfloat16)


def per_device(draws, u_factors, v_factors, ranks, near, row_coords, col_coords):
    rows_local, cols_local, tile, rank = u_factors.shape
    first_col = lax.axis_index("col") * cols_local
    whole = lax.all_gather(draws, "row", axis=0, tiled=True)
    width = whole.shape[0]
    column_ids = first_col + jnp.arange(cols_local, dtype=jnp.int32)
    flagged = jnp.any(near[:, :, None] == column_ids[None, None, :], axis=1)
    keep = (jnp.arange(rank, dtype=jnp.int32)[None, None, :] < ranks[:, :, None]) & jnp.logical_not(
        flagged
    )[:, :, None]
    blocks = whole.reshape(width, cols_local, tile)
    reduced = jnp.einsum("nbt,abtk->nabk", blocks, v_factors, preferred_element_type=jnp.float32)
    reduced = jnp.where(keep[None], reduced, 0.0).astype(jnp.bfloat16)
    partial_value = jnp.einsum(
        "nabk,abtk->nat", reduced, u_factors, preferred_element_type=jnp.float32
    )
    partial_value = partial_value.reshape(width, rows_local * tile)
    local_cols = lax.dynamic_slice_in_dim(col_coords, first_col * tile, cols_local * tile, 1)

    def add_tile(step, total):
        row_pos = step // cols_local
        col_pos = step % cols_local

        def dense(acc):
            tile_matrix = matern_tile(
                lax.dynamic_slice_in_dim(local_cols, col_pos * tile, tile, 1),
                lax.dynamic_slice_in_dim(row_coords, row_pos * tile, tile, 1),
            )
            piece = lax.dynamic_slice_in_dim(whole, col_pos * tile, tile, 1)
            product = jnp.dot(piece, tile_matrix, preferred_element_type=jnp.float32)
            current = lax.dynamic_slice_in_dim(acc, row_pos * tile, tile, 1)
            return lax.dynamic_update_slice_in_dim(acc, current + product, row_pos * tile, 1)

        return lax.cond(flagged[row_pos, col_pos], dense, lambda acc: acc, total)

    partial_value = lax.fori_loop(0, rows_local * cols_local, add_tile, partial_value)
    result = lax.psum_scatter(partial_value, "col", scatter_dimension=0, tiled=True)
    return result


def kernel(
    cols, draws, u_hbm, v_hbm, ranks, near, row_coords, col_coords, out,
    u, v, whole, dense, col_wide, row_terms, red, total, mail, inbox, own,
    factor_sem, gs_sem, gr_sem, ss_sem, sr_sem,
):
    groups, part_rows, width = whole.shape[0], whole.shape[1], whole.shape[2]
    rows_local, cols_local, rank, tile = u.shape
    nrhs = groups * part_rows
    share = nrhs // cols
    chunks = rows_local * tile // WIDE
    per_row = tile // WIDE
    row = lax.axis_index("row")
    col = lax.axis_index("col")
    first = col * cols_local

    sibling = row + 1 - 2 * (row % 2)
    beside = row + 2 - 4 * ((row // 2) % 2)
    above = row + 4 - 8 * ((row // 4) % 2)
    across = beside + 4 - 8 * ((row // 4) % 2)

    def other(index):
        return index + 1 - 2 * (index % 2)

    barrier = pltpu.get_barrier_semaphore()
    for peer in (sibling, beside, above, across):
        pl.semaphore_signal(barrier, inc=1, device_id=(peer, col), device_id_type=MESH)
    for step in range(1, cols):
        pl.semaphore_signal(barrier, inc=1, device_id=(row, (col + step) % cols), device_id_type=MESH)

    u_copy = pltpu.make_async_copy(u_hbm, u, factor_sem.at[0])
    v_copy = pltpu.make_async_copy(v_hbm, v, factor_sem.at[1])
    u_copy.start()
    v_copy.start()

    row_terms[...] = row_coords[...] * LOG2E
    for block in range(width // 128):
        at = pl.multiple_of(first * tile + block * 128, 128)
        for axis in range(2):
            line = col_coords[axis : axis + 1, pl.ds(at, 128)] * LOG2E
            wide = jnp.transpose(jnp.broadcast_to(line, (128, 128)))
            col_wide[axis, block * 128 : (block + 1) * 128, :] = wide
    whole[row] = draws[...]
    pl.semaphore_wait(barrier, 3 + cols)

    def gather(source, slot, peer, index):
        return pltpu.make_async_remote_copy(
            src_ref=source, dst_ref=whole.at[slot], send_sem=gs_sem.at[index],
            recv_sem=gr_sem.at[index], device_id=(peer, col), device_id_type=MESH,
        )

    firsts = [gather(draws, row, peer, index) for index, peer in enumerate((beside, above, across, sibling))]
    for copy in firsts:
        copy.start()

    def gen(chunk, j, quarter):
        span = slice(chunk * WIDE, (chunk + 1) * WIDE)
        row_x, row_y = row_terms[0:1, span], row_terms[1:2, span]
        for part in range(4):
            at = pl.multiple_of(j * tile + quarter * WIDE + part * 64, 64)
            col_x, col_y = col_wide[0, pl.ds(at, 64), :], col_wide[1, pl.ds(at, 64), :]
            delta_x = jnp.concatenate([col_x, col_x], axis=1) - row_x
            delta_y = jnp.concatenate([col_y, col_y], axis=1) - row_y
            squared = jnp.maximum(delta_x * delta_x + delta_y * delta_y, TINY)
            value = jnp.exp2(-(squared * lax.rsqrt(squared)))
            dense[chunk, pl.ds(at, 64), :] = value.astype(jnp.bfloat16)

    def flag(i, j):
        hit = jnp.where(near[i : i + 1, :] == first + j, 1.0, 0.0)
        return jnp.max(hit, axis=1, keepdims=True)

    def mul(chunk, j, quarter):
        at = pl.multiple_of(j * tile + quarter * WIDE, WIDE)
        left = whole[:, :, pl.ds(at, WIDE)].reshape(nrhs, WIDE)
        return jnp.dot(left, dense[chunk, pl.ds(at, WIDE), :], preferred_element_type=jnp.float32)

    def step(makes, takes):
        for take in takes:
            total[take % 2] = jnp.zeros_like(total[take % 2])

        def body(j, carry):
            sums = [None for _ in takes]
            for quarter in range(tile // WIDE):
                for make in makes:
                    gen(make, j, quarter)
                for n, take in enumerate(takes):
                    product = mul(take, j, quarter)
                    sums[n] = product if sums[n] is None else sums[n] + product
            for n, take in enumerate(takes):
                total[take % 2] += sums[n] * flag(take // per_row, j)
            return carry

        lax.fori_loop(0, cols_local, body, 0)
        for take in takes:
            send(take)

    def delivery(chunk, step):
        peer = (col + step) % cols
        return pltpu.make_async_remote_copy(
            src_ref=mail.at[chunk, peer], dst_ref=inbox.at[chunk, step - 1],
            send_sem=ss_sem.at[chunk, step - 1], recv_sem=sr_sem.at[chunk, step - 1],
            device_id=(row, peer), device_id_type=MESH,
        )

    def send(chunk):
        i = chunk // per_row
        base = (chunk % per_row) * WIDE
        value = total[chunk % 2] * 0.03125
        far = u[i, :, :, base : base + WIDE].reshape(cols_local * rank, WIDE)
        value = value + jnp.dot(red[i], far, preferred_element_type=jnp.float32)
        value = value.reshape(cols, share, WIDE)
        mail[chunk] = value.astype(jnp.bfloat16)
        own[chunk] = value
        for step in range(1, cols):
            delivery(chunk, step).start()

    def receive(chunk):
        value = own[chunk, col]
        for step in range(1, cols):
            delivery(chunk, step).wait_recv()
            value = value + inbox[chunk, step - 1].astype(jnp.float32)
        out[:, chunk * WIDE : (chunk + 1) * WIDE] = value

    for phase in PLAN:
        kind = phase[0]
        if kind == "step":
            step(phase[1], phase[2])
        elif kind == "forward":
            for index in phase[1]:
                firsts[index].wait_recv()
                slot = (beside, above, across)[index]
                gather(whole.at[slot], slot, sibling, 4 + index).start()
        elif kind == "ready":
            for index in range(3):
                slot = other((beside, above, across)[index])
                gather(whole.at[slot], slot, sibling, 4 + index).wait_recv()
            firsts[3].wait_recv()
        elif kind == "reduce":
            u_copy.wait()
            v_copy.wait()
            for j in range(cols_local):
                left = whole[:, :, j * tile : (j + 1) * tile].reshape(nrhs, tile)
                for i in range(rows_local):
                    value = lax.dot_general(
                        left, v[i, j], (((1,), (1,)), ((), ())), preferred_element_type=jnp.float32
                    )
                    index = lax.broadcasted_iota(jnp.int32, value.shape, 1)
                    keep = jnp.where(index < ranks[i : i + 1, j : j + 1], 1.0, 0.0) * (1.0 - flag(i, j))
                    red[i, :, j * rank : (j + 1) * rank] = jnp.where(keep > 0.5, value, 0.0).astype(jnp.bfloat16)
        elif kind == "receive":
            for chunk in phase[1]:
                receive(chunk)

    for copy in firsts:
        copy.wait_send()
    for index in range(3):
        slot = (beside, above, across)[index]
        gather(whole.at[slot], slot, sibling, 4 + index).wait_send()
    for chunk in range(chunks):
        for step_at in range(1, cols):
            delivery(chunk, step_at).wait_send()


PLAN = (
    ("step", (0,), ()),
    ("step", (1,), ()),
    ("forward", (0, 1)),
    ("step", (2,), ()),
    ("forward", (2,)),
    ("step", (3,), ()),
    ("ready",),
    ("reduce",),
    ("step", (4,), (0, 1)),
    ("step", (5,), (2, 3)),
    ("step", (6,), (4, 5)),
    ("receive", (0, 1)),
    ("step", (7,), (6,)),
    ("receive", (2, 3)),
    ("step", (), (7,)),
    ("receive", (4, 5, 6, 7)),
)


def fused(rows, cols, draws, u_factors, v_factors, ranks, near, row_coords, col_coords):
    part_rows, width = draws.shape
    rows_local, cols_local, tile, rank = u_factors.shape
    nrhs = part_rows * rows
    share = nrhs // cols
    chunks = rows_local * tile // WIDE
    vmem = pl.BlockSpec(memory_space=pltpu.VMEM)
    hbm = pl.BlockSpec(memory_space=pl.ANY)
    return pl.pallas_call(
        functools.partial(kernel, cols),
        out_shape=jax.ShapeDtypeStruct((share, rows_local * tile), jnp.float32),
        in_specs=[vmem, hbm, hbm, vmem, vmem, vmem, vmem],
        out_specs=vmem,
        scratch_shapes=[
            pltpu.VMEM((rows_local, cols_local, rank, tile), jnp.bfloat16),
            pltpu.VMEM((rows_local, cols_local, rank, tile), jnp.bfloat16),
            pltpu.VMEM((rows, part_rows, width), jnp.bfloat16),
            pltpu.VMEM((chunks, width, WIDE), jnp.bfloat16),
            pltpu.VMEM((2, width, 128), jnp.float32),
            pltpu.VMEM((2, rows_local * tile), jnp.float32),
            pltpu.VMEM((rows_local, nrhs, cols_local * rank), jnp.bfloat16),
            pltpu.VMEM((2, nrhs, WIDE), jnp.float32),
            pltpu.VMEM((chunks, cols, share, WIDE), jnp.bfloat16),
            pltpu.VMEM((chunks, cols - 1, share, WIDE), jnp.bfloat16),
            pltpu.VMEM((chunks, cols, share, WIDE), jnp.float32),
            pltpu.SemaphoreType.DMA((2,)),
            pltpu.SemaphoreType.DMA((7,)),
            pltpu.SemaphoreType.DMA((7,)),
            pltpu.SemaphoreType.DMA((chunks, cols - 1)),
            pltpu.SemaphoreType.DMA((chunks, cols - 1)),
        ],
        compiler_params=pltpu.CompilerParams(
            collective_id=0, has_side_effects=True, vmem_limit_bytes=48 * 1024 * 1024
        ),
        cost_estimate=pl.CostEstimate(flops=10**10, bytes_accessed=10**7, transcendentals=2 * 10**7),
    )(
        draws, jnp.swapaxes(u_factors, 2, 3), jnp.swapaxes(v_factors, 2, 3),
        ranks, near, row_coords, col_coords,
    )


def solution(mesh):
    rows, cols = mesh.shape["row"], mesh.shape["col"]

    def local(*args):
        share = args[0].shape[0] * rows // cols
        if rows == 8 and cols == 4 and args[0].shape[0] % 16 == 0 and share % 16 == 0 and args[1].shape[:3] == (2, 4, 1024):
            return fused(rows, cols, *args)
        return per_device(*args)

    return jax.shard_map(
        local,
        mesh=mesh,
        in_specs=(
            P("row", "col"),
            P("row", "col", None, None),
            P("row", "col", None, None),
            P("row", "col"),
            P("row", None),
            P(None, "row"),
            P(),
        ),
        out_specs=P("col", "row"),
        check_vma=False,
    )
```

```python
import functools

import jax
import jax.numpy as jnp
from jax import lax
from jax.experimental import pallas as pl
from jax.experimental.pallas import tpu as pltpu
from jax.sharding import PartitionSpec as P

MESH = pl.DeviceIdType.MESH
LOG2E = 1.4426950408889634
TINY = 1e-12
WIDE = 256


def matern_tile(col_part, row_part):
    delta_x = col_part[0][:, None] - row_part[0][None, :]
    delta_y = col_part[1][:, None] - row_part[1][None, :]
    kernel = jnp.exp(-jnp.sqrt(delta_x * delta_x + delta_y * delta_y)) * 0.03125
    return kernel.astype(jnp.bfloat16)


def per_device(draws, u_factors, v_factors, ranks, near, row_coords, col_coords):
    rows_local, cols_local, tile, rank = u_factors.shape
    first_col = lax.axis_index("col") * cols_local
    whole = lax.all_gather(draws, "row", axis=0, tiled=True)
    width = whole.shape[0]
    column_ids = first_col + jnp.arange(cols_local, dtype=jnp.int32)
    flagged = jnp.any(near[:, :, None] == column_ids[None, None, :], axis=1)
    keep = (jnp.arange(rank, dtype=jnp.int32)[None, None, :] < ranks[:, :, None]) & jnp.logical_not(
        flagged
    )[:, :, None]
    blocks = whole.reshape(width, cols_local, tile)
    reduced = jnp.einsum("nbt,abtk->nabk", blocks, v_factors, preferred_element_type=jnp.float32)
    reduced = jnp.where(keep[None], reduced, 0.0).astype(jnp.bfloat16)
    partial_value = jnp.einsum(
        "nabk,abtk->nat", reduced, u_factors, preferred_element_type=jnp.float32
    )
    partial_value = partial_value.reshape(width, rows_local * tile)
    local_cols = lax.dynamic_slice_in_dim(col_coords, first_col * tile, cols_local * tile, 1)

    def add_tile(step, total):
        row_pos = step // cols_local
        col_pos = step % cols_local

        def dense(acc):
            tile_matrix = matern_tile(
                lax.dynamic_slice_in_dim(local_cols, col_pos * tile, tile, 1),
                lax.dynamic_slice_in_dim(row_coords, row_pos * tile, tile, 1),
            )
            piece = lax.dynamic_slice_in_dim(whole, col_pos * tile, tile, 1)
            product = jnp.dot(piece, tile_matrix, preferred_element_type=jnp.float32)
            current = lax.dynamic_slice_in_dim(acc, row_pos * tile, tile, 1)
            return lax.dynamic_update_slice_in_dim(acc, current + product, row_pos * tile, 1)

        return lax.cond(flagged[row_pos, col_pos], dense, lambda acc: acc, total)

    partial_value = lax.fori_loop(0, rows_local * cols_local, add_tile, partial_value)
    result = lax.psum_scatter(partial_value, "col", scatter_dimension=0, tiled=True)
    return result


def kernel(
    cols, draws, u_hbm, v_hbm, ranks_hbm, near_hbm, row_hbm, col_hbm, out,
    u, v, ranks, near, row_coords, col_coords, whole, dense, col_wide, row_terms, red_part, red, total, mail, inbox, own,
    factor_sem, gs_sem, gr_sem, ss_sem, sr_sem,
):
    groups, part_rows, width = whole.shape[0], whole.shape[1], whole.shape[2]
    rows_local, cols_local, rank, tile = u.shape
    nrhs = groups * part_rows
    share = nrhs // cols
    chunks = rows_local * tile // WIDE
    per_row = tile // WIDE
    row = lax.axis_index("row")
    col = lax.axis_index("col")
    first = col * cols_local

    sibling = row + 1 - 2 * (row % 2)
    beside = row + 2 - 4 * ((row // 2) % 2)
    above = row + 4 - 8 * ((row // 4) % 2)
    across = beside + 4 - 8 * ((row // 4) % 2)

    def other(index):
        return index + 1 - 2 * (index % 2)

    partner = col + 1 - 2 * (col % 2)
    mirror = cols - 1 - col

    barrier = pltpu.get_barrier_semaphore()
    for peer in (sibling, beside, above, across):
        pl.semaphore_signal(barrier, inc=1, device_id=(peer, col), device_id_type=MESH)
    for peer in (partner, mirror):
        pl.semaphore_signal(barrier, inc=1, device_id=(row, peer), device_id_type=MESH)

    span = pl.ds(pl.multiple_of(first * tile, tile), width)
    pairs = (
        (row_hbm, row_coords), (col_hbm.at[:, span], col_coords), (draws, whole.at[row]),
        (near_hbm, near), (ranks_hbm, ranks), (u_hbm, u), (v_hbm, v),
    )
    fetches = [pltpu.make_async_copy(a, b, factor_sem.at[n]) for n, (a, b) in enumerate(pairs)]
    for fetch in fetches:
        fetch.start()
    fetches[0].wait()
    fetches[1].wait()
    row_terms[...] = row_coords[...] * LOG2E
    for block in range(width // 128):
        for axis in range(2):
            line = col_coords[axis : axis + 1, block * 128 : (block + 1) * 128] * LOG2E
            wide = jnp.transpose(jnp.broadcast_to(line, (128, 128)))
            col_wide[axis, block * 128 : (block + 1) * 128, :] = wide
    pl.semaphore_wait(barrier, 6)

    def gather(source, slot, peer, index):
        return pltpu.make_async_remote_copy(
            src_ref=source, dst_ref=whole.at[slot], send_sem=gs_sem.at[index],
            recv_sem=gr_sem.at[index], device_id=(peer, col), device_id_type=MESH,
        )

    firsts = [gather(draws, row, peer, index) for index, peer in enumerate((beside, above, across, sibling))]
    for copy in firsts:
        copy.start()

    def gen(chunk, j, quarter):
        span = slice(chunk * WIDE, (chunk + 1) * WIDE)
        row_x, row_y = row_terms[0:1, span], row_terms[1:2, span]
        for part in range(4):
            at = pl.multiple_of(j * tile + quarter * WIDE + part * 64, 64)
            col_x, col_y = col_wide[0, pl.ds(at, 64), :], col_wide[1, pl.ds(at, 64), :]
            delta_x = jnp.concatenate([col_x, col_x], axis=1) - row_x
            delta_y = jnp.concatenate([col_y, col_y], axis=1) - row_y
            squared = jnp.maximum(delta_x * delta_x + delta_y * delta_y, TINY)
            value = jnp.exp2(-(squared * lax.rsqrt(squared)))
            dense[chunk, pl.ds(at, 64), :] = value.astype(jnp.bfloat16)

    def flag(i, j):
        hit = jnp.where(near[i : i + 1, :] == first + j, 1.0, 0.0)
        return jnp.max(hit, axis=1, keepdims=True)

    def mul(chunk, j, quarter):
        at = pl.multiple_of(j * tile + quarter * WIDE, WIDE)
        left = whole[:, :, pl.ds(at, WIDE)].reshape(nrhs, WIDE)
        return jnp.dot(left, dense[chunk, pl.ds(at, WIDE), :], preferred_element_type=jnp.float32)

    def reduce(j):
        left = whole[:, :, pl.ds(pl.multiple_of(j * tile, tile), tile)].reshape(nrhs, tile)
        for i in range(rows_local):
            value = lax.dot_general(
                left, v[i, j], (((1,), (1,)), ((), ())), preferred_element_type=jnp.float32
            )
            here = lax.broadcasted_iota(jnp.int32, (1, cols_local), 1) == j
            most = jnp.sum(jnp.where(here, ranks[i : i + 1, :], 0), axis=1, keepdims=True)
            index = lax.broadcasted_iota(jnp.int32, value.shape, 1)
            keep = jnp.where(index < most, 1.0, 0.0) * (1.0 - flag(i, j))
            red_part[i, j] = jnp.where(keep > 0.5, value, 0.0).astype(jnp.bfloat16)

    def step(makes, takes, reduces=False):
        for take in takes:
            total[take % 2] = jnp.zeros_like(total[take % 2])

        def body(j, carry):
            sums = [None for _ in takes]
            if reduces:
                reduce(j)
            for quarter in range(tile // WIDE):
                for make in makes:
                    gen(make, j, quarter)
                for n, take in enumerate(takes):
                    product = mul(take, j, quarter)
                    sums[n] = product if sums[n] is None else sums[n] + product
            for n, take in enumerate(takes):
                total[take % 2] += sums[n] * flag(take // per_row, j)
            return carry

        lax.fori_loop(0, cols_local, body, 0)
        if reduces:
            for i in range(rows_local):
                for j in range(cols_local):
                    red[i, :, j * rank : (j + 1) * rank] = red_part[i, j]
        for take in takes:
            send(take)

    def to_partner(chunk):
        return pltpu.make_async_remote_copy(
            src_ref=mail.at[chunk, pl.ds(0, 2)], dst_ref=inbox.at[chunk, pl.ds(0, 2)],
            send_sem=ss_sem.at[chunk, 0], recv_sem=sr_sem.at[chunk, 0],
            device_id=(row, partner), device_id_type=MESH,
        )

    def to_mirror(chunk):
        return pltpu.make_async_remote_copy(
            src_ref=mail.at[chunk, 2], dst_ref=inbox.at[chunk, 2],
            send_sem=ss_sem.at[chunk, 1], recv_sem=sr_sem.at[chunk, 1],
            device_id=(row, mirror), device_id_type=MESH,
        )

    def send(chunk):
        i = chunk // per_row
        base = (chunk % per_row) * WIDE
        value = total[chunk % 2] * 0.03125
        far = u[i, :, :, base : base + WIDE].reshape(cols_local * rank, WIDE)
        value = value + jnp.dot(red[i], far, preferred_element_type=jnp.float32)
        value = value.reshape(cols, share, WIDE)
        own[chunk] = value
        mail[chunk, 0] = own[chunk, partner].astype(jnp.bfloat16)
        mail[chunk, 1] = own[chunk, cols - 1 - partner].astype(jnp.bfloat16)
        to_partner(chunk).start()

    def relay(chunk):
        to_partner(chunk).wait_recv()
        passed = own[chunk, mirror] + inbox[chunk, 1].astype(jnp.float32)
        mail[chunk, 2] = passed.astype(jnp.bfloat16)
        to_mirror(chunk).start()

    def receive(chunk):
        to_mirror(chunk).wait_recv()
        value = own[chunk, col] + inbox[chunk, 0].astype(jnp.float32)
        out[:, chunk * WIDE : (chunk + 1) * WIDE] = value + inbox[chunk, 2].astype(jnp.float32)

    for phase in PLAN:
        kind = phase[0]
        if kind == "step":
            step(*phase[1:])
        elif kind == "forward":
            for index in phase[1]:
                firsts[index].wait_recv()
                slot = (beside, above, across)[index]
                gather(whole.at[slot], slot, sibling, 4 + index).start()
        elif kind == "ready":
            for index in range(3):
                slot = other((beside, above, across)[index])
                gather(whole.at[slot], slot, sibling, 4 + index).wait_recv()
            firsts[3].wait_recv()
            for fetch in fetches[2:]:
                fetch.wait()
        elif kind == "relay":
            for chunk in phase[1]:
                relay(chunk)
        elif kind == "receive":
            for chunk in phase[1]:
                receive(chunk)

    for copy in firsts:
        copy.wait_send()
    for index in range(3):
        slot = (beside, above, across)[index]
        gather(whole.at[slot], slot, sibling, 4 + index).wait_send()
    for chunk in range(chunks):
        to_partner(chunk).wait_send()
        to_mirror(chunk).wait_send()


PLAN = (
    ("step", (0,), ()),
    ("step", (1,), ()),
    ("forward", (0, 1)),
    ("step", (2,), ()),
    ("forward", (2,)),
    ("ready",),
    ("step", (), (0,), True),
    ("step", (3,), (1, 2)),
    ("relay", (0,)),
    ("step", (4,), (3,)),
    ("relay", (1, 2)),
    ("receive", (0,)),
    ("step", (5,), (4,)),
    ("relay", (3,)),
    ("receive", (1, 2)),
    ("step", (6,), (5,)),
    ("relay", (4,)),
    ("receive", (3,)),
    ("step", (7,), (6,)),
    ("relay", (5,)),
    ("receive", (4,)),
    ("step", (), (7,)),
    ("relay", (6, 7)),
    ("receive", (5, 6, 7)),
)


def fused(rows, cols, draws, u_factors, v_factors, ranks, near, row_coords, col_coords):
    part_rows, width = draws.shape
    rows_local, cols_local, tile, rank = u_factors.shape
    nrhs = part_rows * rows
    share = nrhs // cols
    chunks = rows_local * tile // WIDE
    vmem = pl.BlockSpec(memory_space=pltpu.VMEM)
    hbm = pl.BlockSpec(memory_space=pl.ANY)
    return pl.pallas_call(
        functools.partial(kernel, cols),
        out_shape=jax.ShapeDtypeStruct((share, rows_local * tile), jnp.float32),
        in_specs=[hbm] * 7,
        out_specs=vmem,
        scratch_shapes=[
            pltpu.VMEM((rows_local, cols_local, rank, tile), jnp.bfloat16),
            pltpu.VMEM((rows_local, cols_local, rank, tile), jnp.bfloat16),
            pltpu.VMEM(ranks.shape, jnp.int32),
            pltpu.VMEM(near.shape, jnp.int32),
            pltpu.VMEM(row_coords.shape, jnp.float32),
            pltpu.VMEM((2, width), jnp.float32),
            pltpu.VMEM((rows, part_rows, width), jnp.bfloat16),
            pltpu.VMEM((chunks, width, WIDE), jnp.bfloat16),
            pltpu.VMEM((2, width, 128), jnp.float32),
            pltpu.VMEM((2, rows_local * tile), jnp.float32),
            pltpu.VMEM((rows_local, cols_local, nrhs, rank), jnp.bfloat16),
            pltpu.VMEM((rows_local, nrhs, cols_local * rank), jnp.bfloat16),
            pltpu.VMEM((2, nrhs, WIDE), jnp.float32),
            pltpu.VMEM((chunks, 3, share, WIDE), jnp.bfloat16),
            pltpu.VMEM((chunks, 3, share, WIDE), jnp.bfloat16),
            pltpu.VMEM((chunks, cols, share, WIDE), jnp.float32),
            pltpu.SemaphoreType.DMA((7,)),
            pltpu.SemaphoreType.DMA((7,)),
            pltpu.SemaphoreType.DMA((7,)),
            pltpu.SemaphoreType.DMA((chunks, 2)),
            pltpu.SemaphoreType.DMA((chunks, 2)),
        ],
        compiler_params=pltpu.CompilerParams(
            collective_id=0, has_side_effects=True, vmem_limit_bytes=60 * 1024 * 1024
        ),
        cost_estimate=pl.CostEstimate(flops=10**10, bytes_accessed=10**7, transcendentals=2 * 10**7),
    )(
        draws, jnp.swapaxes(u_factors, 2, 3), jnp.swapaxes(v_factors, 2, 3),
        ranks, near, row_coords, col_coords,
    )


def solution(mesh):
    rows, cols = mesh.shape["row"], mesh.shape["col"]

    def local(*args):
        share = args[0].shape[0] * rows // cols
        if rows == 8 and cols == 4 and args[0].shape[0] % 16 == 0 and share % 16 == 0 and args[1].shape[:3] == (2, 4, 1024):
            return fused(rows, cols, *args)
        return per_device(*args)

    return jax.shard_map(
        local,
        mesh=mesh,
        in_specs=(
            P("row", "col"),
            P("row", "col", None, None),
            P("row", "col", None, None),
            P("row", "col"),
            P("row", None),
            P(None, "row"),
            P(),
        ),
        out_specs=P("col", "row"),
        check_vma=False,
    )
```

```python
import functools

import jax
import jax.numpy as jnp
from jax import lax
from jax.experimental import pallas as pl
from jax.experimental.pallas import tpu as pltpu
from jax.sharding import PartitionSpec as P

MESH = pl.DeviceIdType.MESH
LOG2E = 1.4426950408889634
TINY = 1e-12
WIDE = 256


def matern_tile(col_part, row_part):
    delta_x = col_part[0][:, None] - row_part[0][None, :]
    delta_y = col_part[1][:, None] - row_part[1][None, :]
    kernel = jnp.exp(-jnp.sqrt(delta_x * delta_x + delta_y * delta_y)) * 0.03125
    return kernel.astype(jnp.bfloat16)


def per_device(draws, u_factors, v_factors, ranks, near, row_coords, col_coords):
    rows_local, cols_local, tile, rank = u_factors.shape
    first_col = lax.axis_index("col") * cols_local
    whole = lax.all_gather(draws, "row", axis=0, tiled=True)
    width = whole.shape[0]
    column_ids = first_col + jnp.arange(cols_local, dtype=jnp.int32)
    flagged = jnp.any(near[:, :, None] == column_ids[None, None, :], axis=1)
    keep = (jnp.arange(rank, dtype=jnp.int32)[None, None, :] < ranks[:, :, None]) & jnp.logical_not(
        flagged
    )[:, :, None]
    blocks = whole.reshape(width, cols_local, tile)
    reduced = jnp.einsum("nbt,abtk->nabk", blocks, v_factors, preferred_element_type=jnp.float32)
    reduced = jnp.where(keep[None], reduced, 0.0).astype(jnp.bfloat16)
    partial_value = jnp.einsum(
        "nabk,abtk->nat", reduced, u_factors, preferred_element_type=jnp.float32
    )
    partial_value = partial_value.reshape(width, rows_local * tile)
    local_cols = lax.dynamic_slice_in_dim(col_coords, first_col * tile, cols_local * tile, 1)

    def add_tile(step, total):
        row_pos = step // cols_local
        col_pos = step % cols_local

        def dense(acc):
            tile_matrix = matern_tile(
                lax.dynamic_slice_in_dim(local_cols, col_pos * tile, tile, 1),
                lax.dynamic_slice_in_dim(row_coords, row_pos * tile, tile, 1),
            )
            piece = lax.dynamic_slice_in_dim(whole, col_pos * tile, tile, 1)
            product = jnp.dot(piece, tile_matrix, preferred_element_type=jnp.float32)
            current = lax.dynamic_slice_in_dim(acc, row_pos * tile, tile, 1)
            return lax.dynamic_update_slice_in_dim(acc, current + product, row_pos * tile, 1)

        return lax.cond(flagged[row_pos, col_pos], dense, lambda acc: acc, total)

    partial_value = lax.fori_loop(0, rows_local * cols_local, add_tile, partial_value)
    result = lax.psum_scatter(partial_value, "col", scatter_dimension=0, tiled=True)
    return result


def split3(value):
    high = value.astype(jnp.bfloat16).astype(jnp.float32)
    rest = value - high
    middle = rest.astype(jnp.bfloat16).astype(jnp.float32)
    return high, middle, rest - middle


def kernel(
    cols, draws, u_hbm, v_hbm, ranks_hbm, near_hbm, row_hbm, col_hbm, out,
    u, v, ranks, near, row_coords, col_coords, whole, dense, terms, col_wide, row_terms, red_part, red, total, mail, inbox, own,
    factor_sem, gs_sem, gr_sem, ss_sem, sr_sem,
):
    groups, part_rows, width = whole.shape[0], whole.shape[1], whole.shape[2]
    rows_local, cols_local, rank, tile = u.shape
    nrhs = groups * part_rows
    share = nrhs // cols
    chunks = rows_local * tile // WIDE
    per_row = tile // WIDE
    row = lax.axis_index("row")
    col = lax.axis_index("col")
    first = col * cols_local

    sibling = row + 1 - 2 * (row % 2)
    beside = row + 2 - 4 * ((row // 2) % 2)
    above = row + 4 - 8 * ((row // 4) % 2)
    across = beside + 4 - 8 * ((row // 4) % 2)

    def other(index):
        return index + 1 - 2 * (index % 2)

    barrier = pltpu.get_barrier_semaphore()
    for peer in (sibling, beside, above, across):
        pl.semaphore_signal(barrier, inc=1, device_id=(peer, col), device_id_type=MESH)
    for hop in range(1, cols):
        pl.semaphore_signal(barrier, inc=1, device_id=(row, (col + hop) % cols), device_id_type=MESH)

    span = pl.ds(pl.multiple_of(first * tile, tile), width)
    pairs = (
        (row_hbm, row_coords), (col_hbm.at[:, span], col_coords), (draws, whole.at[row]),
        (near_hbm, near), (ranks_hbm, ranks), (u_hbm, u), (v_hbm, v),
    )
    fetches = [pltpu.make_async_copy(a, b, factor_sem.at[n]) for n, (a, b) in enumerate(pairs)]
    for fetch in fetches:
        fetch.start()
    fetches[0].wait()
    fetches[1].wait()
    row_terms[...] = row_coords[...] * LOG2E
    terms[...] = jnp.zeros_like(terms)
    line = lax.broadcasted_iota(jnp.int32, (16, 256), 0)
    lane = lax.broadcasted_iota(jnp.int32, (16, 256), 1)
    ones = jnp.where((line < 6) & ((line < 3) == (lane < 128)), 1.0, 0.0).astype(jnp.bfloat16)
    for axis in range(2):
        parts = split3(col_coords[axis : axis + 1, :] * LOG2E)
        for piece in range(3):
            terms[3 * axis + piece : 3 * axis + piece + 1, :] = parts[piece]
    for block in range(width // 512):
        at = slice(block * 512, (block + 1) * 512)
        wide = lax.dot_general(
            terms[:, at].astype(jnp.bfloat16), ones, (((0,), (0,)), ((), ())),
            preferred_element_type=jnp.float32,
        )
        col_wide[0, at, :] = wide[:, :128]
        col_wide[1, at, :] = wide[:, 128:]
    pl.semaphore_wait(barrier, 3 + cols)

    def gather(source, slot, peer, index):
        return pltpu.make_async_remote_copy(
            src_ref=source, dst_ref=whole.at[slot], send_sem=gs_sem.at[index],
            recv_sem=gr_sem.at[index], device_id=(peer, col), device_id_type=MESH,
        )

    firsts = [gather(draws, row, peer, index) for index, peer in enumerate((beside, above, across, sibling))]
    for copy in firsts:
        copy.start()

    def gen(chunk, j, quarter):
        span = slice(chunk * WIDE, (chunk + 1) * WIDE)
        row_x, row_y = row_terms[0:1, span], row_terms[1:2, span]
        for part in range(4):
            at = pl.multiple_of(j * tile + quarter * WIDE + part * 64, 64)
            col_x, col_y = col_wide[0, pl.ds(at, 64), :], col_wide[1, pl.ds(at, 64), :]
            delta_x = jnp.concatenate([col_x, col_x], axis=1) - row_x
            delta_y = jnp.concatenate([col_y, col_y], axis=1) - row_y
            squared = jnp.maximum(delta_x * delta_x + delta_y * delta_y, TINY)
            value = jnp.exp2(-(squared * lax.rsqrt(squared)))
            dense[chunk][pl.ds(at, 64), :] = value.astype(jnp.bfloat16)

    def flag(i, j):
        hit = jnp.where(near[i : i + 1, :] == first + j, 1.0, 0.0)
        return jnp.max(hit, axis=1, keepdims=True)

    def mul(chunk, j):
        span = pl.ds(pl.multiple_of(j * tile, tile), tile)
        left = whole[:, :, span].reshape(nrhs, tile)
        return jnp.dot(left, dense[chunk][span, :], preferred_element_type=jnp.float32)

    def reduce(j):
        left = whole[:, :, pl.ds(pl.multiple_of(j * tile, tile), tile)].reshape(nrhs, tile)
        for i in range(rows_local):
            value = lax.dot_general(
                left, v[i, j], (((1,), (1,)), ((), ())), preferred_element_type=jnp.float32
            )
            here = lax.broadcasted_iota(jnp.int32, (1, cols_local), 1) == j
            most = jnp.sum(jnp.where(here, ranks[i : i + 1, :], 0), axis=1, keepdims=True)
            index = lax.broadcasted_iota(jnp.int32, value.shape, 1)
            keep = jnp.where(index < most, 1.0, 0.0) * (1.0 - flag(i, j))
            red_part[i, j] = jnp.where(keep > 0.5, value, 0.0).astype(jnp.bfloat16)

    def step(makes, takes, reduces=False):
        for take in takes:
            total[take % 2] = jnp.zeros_like(total[take % 2])

        def body(j, carry):
            if reduces:
                reduce(j)
            sums = [mul(take, j) for take in takes]
            for quarter in range(tile // WIDE):
                for make in makes:
                    gen(make, j, quarter)
            for n, take in enumerate(takes):
                total[take % 2] += sums[n] * flag(take // per_row, j)
            return carry

        lax.fori_loop(0, cols_local, body, 0)
        if reduces:
            for i in range(rows_local):
                for j in range(cols_local):
                    red[i, :, j * rank : (j + 1) * rank] = red_part[i, j]
        for take in takes:
            send(take)

    def delivery(chunk, step):
        peer = (col + step) % cols
        return pltpu.make_async_remote_copy(
            src_ref=mail.at[chunk, peer], dst_ref=inbox.at[chunk, step - 1],
            send_sem=ss_sem.at[chunk, step - 1], recv_sem=sr_sem.at[chunk, step - 1],
            device_id=(row, peer), device_id_type=MESH,
        )

    def send(chunk):
        i = chunk // per_row
        base = (chunk % per_row) * WIDE
        value = total[chunk % 2] * 0.03125
        far = u[i, :, :, base : base + WIDE].reshape(cols_local * rank, WIDE)
        value = value + jnp.dot(red[i], far, preferred_element_type=jnp.float32)
        value = value.reshape(cols, share, WIDE)
        mail[chunk] = value.astype(jnp.bfloat16)
        own[chunk] = value
        for step in range(1, cols):
            delivery(chunk, step).start()

    def receive(chunk):
        value = own[chunk, col]
        for step in range(1, cols):
            delivery(chunk, step).wait_recv()
            value = value + inbox[chunk, step - 1].astype(jnp.float32)
        out[:, chunk * WIDE : (chunk + 1) * WIDE] = value

    for phase in PLAN:
        kind = phase[0]
        if kind == "step":
            step(*phase[1:])
        elif kind == "forward":
            for index in phase[1]:
                firsts[index].wait_recv()
                slot = (beside, above, across)[index]
                gather(whole.at[slot], slot, sibling, 4 + index).start()
        elif kind == "ready":
            for index in range(3):
                slot = other((beside, above, across)[index])
                gather(whole.at[slot], slot, sibling, 4 + index).wait_recv()
            firsts[3].wait_recv()
            for fetch in fetches[2:]:
                fetch.wait()
        elif kind == "receive":
            for chunk in phase[1]:
                receive(chunk)

    for copy in firsts:
        copy.wait_send()
    for index in range(3):
        slot = (beside, above, across)[index]
        gather(whole.at[slot], slot, sibling, 4 + index).wait_send()
    for chunk in range(chunks):
        for step_at in range(1, cols):
            delivery(chunk, step_at).wait_send()


PLAN = (
    ("step", (0,), ()),
    ("step", (1,), ()),
    ("forward", (0, 1)),
    ("step", (2,), ()),
    ("forward", (2,)),
    ("step", (3,), ()),
    ("ready",),
    ("step", (4,), (0, 1), True),
    ("step", (5,), (2, 3)),
    ("step", (6,), (4, 5)),
    ("receive", (0, 1)),
    ("step", (7,), (6,)),
    ("receive", (2, 3)),
    ("step", (), (7,)),
    ("receive", (4, 5, 6, 7)),
)


def fused(rows, cols, draws, u_factors, v_factors, ranks, near, row_coords, col_coords):
    part_rows, width = draws.shape
    rows_local, cols_local, tile, rank = u_factors.shape
    nrhs = part_rows * rows
    share = nrhs // cols
    chunks = rows_local * tile // WIDE
    vmem = pl.BlockSpec(memory_space=pltpu.VMEM)
    hbm = pl.BlockSpec(memory_space=pl.ANY)
    return pl.pallas_call(
        functools.partial(kernel, cols),
        out_shape=jax.ShapeDtypeStruct((share, rows_local * tile), jnp.float32),
        in_specs=[hbm] * 7,
        out_specs=vmem,
        scratch_shapes=[
            pltpu.VMEM((rows_local, cols_local, rank, tile), jnp.bfloat16),
            pltpu.VMEM((rows_local, cols_local, rank, tile), jnp.bfloat16),
            pltpu.VMEM(ranks.shape, jnp.int32),
            pltpu.VMEM(near.shape, jnp.int32),
            pltpu.VMEM(row_coords.shape, jnp.float32),
            pltpu.VMEM((2, width), jnp.float32),
            pltpu.VMEM((rows, part_rows, width), jnp.bfloat16),
            [pltpu.VMEM((width, WIDE), jnp.bfloat16) for _ in range(chunks)],
            pltpu.VMEM((16, width), jnp.float32),
            pltpu.VMEM((2, width, 128), jnp.float32),
            pltpu.VMEM((2, rows_local * tile), jnp.float32),
            pltpu.VMEM((rows_local, cols_local, nrhs, rank), jnp.bfloat16),
            pltpu.VMEM((rows_local, nrhs, cols_local * rank), jnp.bfloat16),
            pltpu.VMEM((2, nrhs, WIDE), jnp.float32),
            pltpu.VMEM((chunks, cols, share, WIDE), jnp.bfloat16),
            pltpu.VMEM((chunks, cols - 1, share, WIDE), jnp.bfloat16),
            pltpu.VMEM((chunks, cols, share, WIDE), jnp.float32),
            pltpu.SemaphoreType.DMA((7,)),
            pltpu.SemaphoreType.DMA((7,)),
            pltpu.SemaphoreType.DMA((7,)),
            pltpu.SemaphoreType.DMA((chunks, cols - 1)),
            pltpu.SemaphoreType.DMA((chunks, cols - 1)),
        ],
        compiler_params=pltpu.CompilerParams(
            collective_id=0, has_side_effects=True, vmem_limit_bytes=60 * 1024 * 1024
        ),
        cost_estimate=pl.CostEstimate(flops=10**10, bytes_accessed=10**7, transcendentals=2 * 10**7),
    )(
        draws, jnp.swapaxes(u_factors, 2, 3), jnp.swapaxes(v_factors, 2, 3),
        ranks, near, row_coords, col_coords,
    )


def solution(mesh):
    rows, cols = mesh.shape["row"], mesh.shape["col"]

    def local(*args):
        share = args[0].shape[0] * rows // cols
        if rows == 8 and cols == 4 and args[0].shape[0] % 16 == 0 and share % 16 == 0 and args[1].shape[:3] == (2, 4, 1024):
            return fused(rows, cols, *args)
        return per_device(*args)

    return jax.shard_map(
        local,
        mesh=mesh,
        in_specs=(
            P("row", "col"),
            P("row", "col", None, None),
            P("row", "col", None, None),
            P("row", "col"),
            P("row", None),
            P(None, "row"),
            P(),
        ),
        out_specs=P("col", "row"),
        check_vma=False,
    )
```

```python
import functools

import jax
import jax.numpy as jnp
from jax import lax
from jax.experimental import pallas as pl
from jax.experimental.pallas import tpu as pltpu
from jax.sharding import PartitionSpec as P

MESH = pl.DeviceIdType.MESH
LOG2E = 1.4426950408889634
TINY = 1e-12
WIDE = 256


def matern_tile(col_part, row_part):
    delta_x = col_part[0][:, None] - row_part[0][None, :]
    delta_y = col_part[1][:, None] - row_part[1][None, :]
    kernel = jnp.exp(-jnp.sqrt(delta_x * delta_x + delta_y * delta_y)) * 0.03125
    return kernel.astype(jnp.bfloat16)


def per_device(draws, u_factors, v_factors, ranks, near, row_coords, col_coords):
    rows_local, cols_local, tile, rank = u_factors.shape
    first_col = lax.axis_index("col") * cols_local
    whole = lax.all_gather(draws, "row", axis=0, tiled=True)
    width = whole.shape[0]
    column_ids = first_col + jnp.arange(cols_local, dtype=jnp.int32)
    flagged = jnp.any(near[:, :, None] == column_ids[None, None, :], axis=1)
    keep = (jnp.arange(rank, dtype=jnp.int32)[None, None, :] < ranks[:, :, None]) & jnp.logical_not(
        flagged
    )[:, :, None]
    blocks = whole.reshape(width, cols_local, tile)
    reduced = jnp.einsum("nbt,abtk->nabk", blocks, v_factors, preferred_element_type=jnp.float32)
    reduced = jnp.where(keep[None], reduced, 0.0).astype(jnp.bfloat16)
    partial_value = jnp.einsum(
        "nabk,abtk->nat", reduced, u_factors, preferred_element_type=jnp.float32
    )
    partial_value = partial_value.reshape(width, rows_local * tile)
    local_cols = lax.dynamic_slice_in_dim(col_coords, first_col * tile, cols_local * tile, 1)

    def add_tile(step, total):
        row_pos = step // cols_local
        col_pos = step % cols_local

        def dense(acc):
            tile_matrix = matern_tile(
                lax.dynamic_slice_in_dim(local_cols, col_pos * tile, tile, 1),
                lax.dynamic_slice_in_dim(row_coords, row_pos * tile, tile, 1),
            )
            piece = lax.dynamic_slice_in_dim(whole, col_pos * tile, tile, 1)
            product = jnp.dot(piece, tile_matrix, preferred_element_type=jnp.float32)
            current = lax.dynamic_slice_in_dim(acc, row_pos * tile, tile, 1)
            return lax.dynamic_update_slice_in_dim(acc, current + product, row_pos * tile, 1)

        return lax.cond(flagged[row_pos, col_pos], dense, lambda acc: acc, total)

    partial_value = lax.fori_loop(0, rows_local * cols_local, add_tile, partial_value)
    result = lax.psum_scatter(partial_value, "col", scatter_dimension=0, tiled=True)
    return result


def split3(value):
    high = value.astype(jnp.bfloat16).astype(jnp.float32)
    rest = value - high
    middle = rest.astype(jnp.bfloat16).astype(jnp.float32)
    return high, middle, rest - middle


def kernel(
    cols, draws, u_hbm, v_hbm, ranks_hbm, near_hbm, row_hbm, col_hbm, out,
    u, v, ranks, near, row_coords, col_coords, whole, dense, terms, col_wide, row_terms, red_part, red, total, mail, inbox, own,
    factor_sem, gs_sem, gr_sem, ss_sem, sr_sem,
):
    groups, part_rows, width = whole.shape[0], whole.shape[1], whole.shape[2]
    rows_local, cols_local, rank, tile = u.shape
    nrhs = groups * part_rows
    share = nrhs // cols
    chunks = rows_local * tile // WIDE
    per_row = tile // WIDE
    row = lax.axis_index("row")
    col = lax.axis_index("col")
    first = col * cols_local

    sibling = row + 1 - 2 * (row % 2)
    beside = row + 2 - 4 * ((row // 2) % 2)
    above = row + 4 - 8 * ((row // 4) % 2)
    across = beside + 4 - 8 * ((row // 4) % 2)

    partner = col + 1 - 2 * (col % 2)
    mirror = cols - 1 - col

    barrier = pltpu.get_barrier_semaphore()
    for peer in (sibling, beside, above):
        pl.semaphore_signal(barrier, inc=1, device_id=(peer, col), device_id_type=MESH)
    for peer in (partner, mirror):
        pl.semaphore_signal(barrier, inc=1, device_id=(row, peer), device_id_type=MESH)

    span = pl.ds(pl.multiple_of(first * tile, tile), width)
    pairs = (
        (row_hbm, row_coords), (col_hbm.at[:, span], col_coords), (draws, whole.at[row]),
        (near_hbm, near), (ranks_hbm, ranks), (u_hbm, u), (v_hbm, v),
    )
    fetches = [pltpu.make_async_copy(a, b, factor_sem.at[n]) for n, (a, b) in enumerate(pairs)]
    for fetch in fetches:
        fetch.start()
    fetches[0].wait()
    fetches[1].wait()
    row_terms[...] = row_coords[...] * LOG2E
    terms[...] = jnp.zeros_like(terms)
    line = lax.broadcasted_iota(jnp.int32, (16, 256), 0)
    lane = lax.broadcasted_iota(jnp.int32, (16, 256), 1)
    ones = jnp.where((line < 6) & ((line < 3) == (lane < 128)), 1.0, 0.0).astype(jnp.bfloat16)
    for axis in range(2):
        parts = split3(col_coords[axis : axis + 1, :] * LOG2E)
        for piece in range(3):
            terms[3 * axis + piece : 3 * axis + piece + 1, :] = parts[piece]
    for block in range(width // 512):
        at = slice(block * 512, (block + 1) * 512)
        wide = lax.dot_general(
            terms[:, at].astype(jnp.bfloat16), ones, (((0,), (0,)), ((), ())),
            preferred_element_type=jnp.float32,
        )
        col_wide[0, at, :] = wide[:, :128]
        col_wide[1, at, :] = wide[:, 128:]
    pl.semaphore_wait(barrier, 5)

    def gather(source, target, peer, index):
        return pltpu.make_async_remote_copy(
            src_ref=source, dst_ref=target, send_sem=gs_sem.at[index],
            recv_sem=gr_sem.at[index], device_id=(peer, col), device_id_type=MESH,
        )

    def half(slot, which):
        return whole.at[slot, :, pl.ds(which * (width // 2), width // 2)]

    def hop(which):
        slot, peer = ((beside, above), (above, beside))[which]
        return gather(half(slot, which), half(slot, which), peer, 2 + 5 * which)

    def pass_on(index):
        slot = (beside, above, across)[index]
        return gather(whole.at[slot], whole.at[slot], sibling, 4 + index)

    firsts = [
        gather(draws, whole.at[row], peer, index)
        for peer, index in ((beside, 0), (above, 1), (sibling, 3))
    ]
    for copy in firsts:
        copy.start()

    def gen(chunk, j, quarter):
        span = slice(chunk * WIDE, (chunk + 1) * WIDE)
        row_x, row_y = row_terms[0:1, span], row_terms[1:2, span]
        for part in range(4):
            at = pl.multiple_of(j * tile + quarter * WIDE + part * 64, 64)
            col_x, col_y = col_wide[0, pl.ds(at, 64), :], col_wide[1, pl.ds(at, 64), :]
            delta_x = jnp.concatenate([col_x, col_x], axis=1) - row_x
            delta_y = jnp.concatenate([col_y, col_y], axis=1) - row_y
            squared = jnp.maximum(delta_x * delta_x + delta_y * delta_y, TINY)
            value = jnp.exp2(-(squared * lax.rsqrt(squared)))
            dense[chunk][pl.ds(at, 64), :] = value.astype(jnp.bfloat16)

    def flag(i, j):
        hit = jnp.where(near[i : i + 1, :] == first + j, 1.0, 0.0)
        return jnp.max(hit, axis=1, keepdims=True)

    def mul(chunk, j):
        span = pl.ds(pl.multiple_of(j * tile, tile), tile)
        left = whole[:, :, span].reshape(nrhs, tile)
        return jnp.dot(left, dense[chunk][span, :], preferred_element_type=jnp.float32)

    def reduce(j):
        left = whole[:, :, pl.ds(pl.multiple_of(j * tile, tile), tile)].reshape(nrhs, tile)
        for i in range(rows_local):
            value = lax.dot_general(
                left, v[i, j], (((1,), (1,)), ((), ())), preferred_element_type=jnp.float32
            )
            here = lax.broadcasted_iota(jnp.int32, (1, cols_local), 1) == j
            most = jnp.sum(jnp.where(here, ranks[i : i + 1, :], 0), axis=1, keepdims=True)
            index = lax.broadcasted_iota(jnp.int32, value.shape, 1)
            keep = jnp.where(index < most, 1.0, 0.0) * (1.0 - flag(i, j))
            red_part[i, j] = jnp.where(keep > 0.5, value, 0.0).astype(jnp.bfloat16)

    def step(makes, takes, reduces=False):
        for take in takes:
            total[take % 2] = jnp.zeros_like(total[take % 2])

        def body(j, carry):
            if reduces:
                reduce(j)
            sums = [mul(take, j) for take in takes]
            for quarter in range(tile // WIDE):
                for make in makes:
                    gen(make, j, quarter)
            for n, take in enumerate(takes):
                total[take % 2] += sums[n] * flag(take // per_row, j)
            return carry

        lax.fori_loop(0, cols_local, body, 0)
        if reduces:
            for i in range(rows_local):
                for j in range(cols_local):
                    red[i, :, j * rank : (j + 1) * rank] = red_part[i, j]
        for take in takes:
            send(take)

    def to_partner(chunk):
        return pltpu.make_async_remote_copy(
            src_ref=mail.at[chunk, pl.ds(0, 2)], dst_ref=inbox.at[chunk, pl.ds(0, 2)],
            send_sem=ss_sem.at[chunk, 0], recv_sem=sr_sem.at[chunk, 0],
            device_id=(row, partner), device_id_type=MESH,
        )

    def to_mirror(chunk):
        return pltpu.make_async_remote_copy(
            src_ref=mail.at[chunk, 2], dst_ref=inbox.at[chunk, 2],
            send_sem=ss_sem.at[chunk, 1], recv_sem=sr_sem.at[chunk, 1],
            device_id=(row, mirror), device_id_type=MESH,
        )

    def send(chunk):
        i = chunk // per_row
        base = (chunk % per_row) * WIDE
        value = total[chunk % 2] * 0.03125
        far = u[i, :, :, base : base + WIDE].reshape(cols_local * rank, WIDE)
        value = value + jnp.dot(red[i], far, preferred_element_type=jnp.float32)
        value = value.reshape(cols, share, WIDE)
        own[chunk] = value
        mail[chunk, 0] = own[chunk, partner].astype(jnp.bfloat16)
        mail[chunk, 1] = own[chunk, cols - 1 - partner].astype(jnp.bfloat16)
        to_partner(chunk).start()

    def relay(chunk):
        to_partner(chunk).wait_recv()
        passed = own[chunk, mirror] + inbox[chunk, 1].astype(jnp.float32)
        mail[chunk, 2] = passed.astype(jnp.bfloat16)
        to_mirror(chunk).start()

    def receive(chunk):
        to_mirror(chunk).wait_recv()
        value = own[chunk, col] + inbox[chunk, 0].astype(jnp.float32)
        out[:, chunk * WIDE : (chunk + 1) * WIDE] = value + inbox[chunk, 2].astype(jnp.float32)

    for phase in PLAN:
        kind = phase[0]
        if kind == "step":
            step(*phase[1:])
        elif kind == "forward":
            for index in range(2):
                firsts[index].wait_recv()
                hop(index).start()
                pass_on(index).start()
        elif kind == "corner":
            for which in range(2):
                hop(which).wait_recv()
            pass_on(2).start()
        elif kind == "ready":
            for index in range(3):
                pass_on(index).wait_recv()
            firsts[2].wait_recv()
            for fetch in fetches[2:]:
                fetch.wait()
        elif kind == "relay":
            for chunk in phase[1]:
                relay(chunk)
        elif kind == "receive":
            for chunk in phase[1]:
                receive(chunk)

    for copy in firsts:
        copy.wait_send()
    for which in range(2):
        hop(which).wait_send()
    for index in range(3):
        pass_on(index).wait_send()
    for chunk in range(chunks):
        to_partner(chunk).wait_send()
        to_mirror(chunk).wait_send()


PLAN = (
    ("step", (0,), ()),
    ("step", (1,), ()),
    ("forward",),
    ("step", (2,), ()),
    ("corner",),
    ("ready",),
    ("step", (), (0, 1), True),
    ("step", (3,), (2,)),
    ("step", (4,), (3,)),
    ("relay", (0, 1)),
    ("step", (5,), (4,)),
    ("relay", (2,)),
    ("step", (6,), (5,)),
    ("relay", (3,)),
    ("receive", (0, 1)),
    ("step", (7,), (6,)),
    ("relay", (4, 5)),
    ("step", (), (7,)),
    ("receive", (2, 3)),
    ("relay", (6, 7)),
    ("receive", (4, 5, 6, 7)),
)


def fused(rows, cols, draws, u_factors, v_factors, ranks, near, row_coords, col_coords):
    part_rows, width = draws.shape
    rows_local, cols_local, tile, rank = u_factors.shape
    nrhs = part_rows * rows
    share = nrhs // cols
    chunks = rows_local * tile // WIDE
    vmem = pl.BlockSpec(memory_space=pltpu.VMEM)
    hbm = pl.BlockSpec(memory_space=pl.ANY)
    return pl.pallas_call(
        functools.partial(kernel, cols),
        out_shape=jax.ShapeDtypeStruct((share, rows_local * tile), jnp.float32),
        in_specs=[hbm] * 7,
        out_specs=vmem,
        scratch_shapes=[
            pltpu.VMEM((rows_local, cols_local, rank, tile), jnp.bfloat16),
            pltpu.VMEM((rows_local, cols_local, rank, tile), jnp.bfloat16),
            pltpu.VMEM(ranks.shape, jnp.int32),
            pltpu.VMEM(near.shape, jnp.int32),
            pltpu.VMEM(row_coords.shape, jnp.float32),
            pltpu.VMEM((2, width), jnp.float32),
            pltpu.VMEM((rows, part_rows, width), jnp.bfloat16),
            [pltpu.VMEM((width, WIDE), jnp.bfloat16) for _ in range(chunks)],
            pltpu.VMEM((16, width), jnp.float32),
            pltpu.VMEM((2, width, 128), jnp.float32),
            pltpu.VMEM((2, rows_local * tile), jnp.float32),
            pltpu.VMEM((rows_local, cols_local, nrhs, rank), jnp.bfloat16),
            pltpu.VMEM((rows_local, nrhs, cols_local * rank), jnp.bfloat16),
            pltpu.VMEM((2, nrhs, WIDE), jnp.float32),
            pltpu.VMEM((chunks, 3, share, WIDE), jnp.bfloat16),
            pltpu.VMEM((chunks, 3, share, WIDE), jnp.bfloat16),
            pltpu.VMEM((chunks, cols, share, WIDE), jnp.float32),
            pltpu.SemaphoreType.DMA((7,)),
            pltpu.SemaphoreType.DMA((8,)),
            pltpu.SemaphoreType.DMA((8,)),
            pltpu.SemaphoreType.DMA((chunks, 2)),
            pltpu.SemaphoreType.DMA((chunks, 2)),
        ],
        compiler_params=pltpu.CompilerParams(
            collective_id=0, has_side_effects=True, vmem_limit_bytes=60 * 1024 * 1024
        ),
        cost_estimate=pl.CostEstimate(flops=10**10, bytes_accessed=10**7, transcendentals=2 * 10**7),
    )(
        draws, jnp.swapaxes(u_factors, 2, 3), jnp.swapaxes(v_factors, 2, 3),
        ranks, near, row_coords, col_coords,
    )


def solution(mesh):
    rows, cols = mesh.shape["row"], mesh.shape["col"]

    def local(*args):
        share = args[0].shape[0] * rows // cols
        if rows == 8 and cols == 4 and args[0].shape[0] % 16 == 0 and share % 16 == 0 and args[1].shape[:3] == (2, 4, 1024):
            return fused(rows, cols, *args)
        return per_device(*args)

    return jax.shard_map(
        local,
        mesh=mesh,
        in_specs=(
            P("row", "col"),
            P("row", "col", None, None),
            P("row", "col", None, None),
            P("row", "col"),
            P("row", None),
            P(None, "row"),
            P(),
        ),
        out_specs=P("col", "row"),
        check_vma=False,
    )
```
